512 devices in a mesh: dp: 32 (over z_hi, y, core), tensor: 16 (over x, z_lo).
Axes of the slice: x: 4, y: 4, z: 16 (z_hi: 4, z_lo: 4; z = z_hi * 4 + z_lo), core: 2. Of those that a mesh axis runs over, the one named last changes fastest.
Arguments:
- gate_in: bfloat16 [4096, 14336], P('dp', 'tensor'), may hold values from -8 to 8
- up_in: bfloat16 [4096, 14336], P('dp', 'tensor'), may hold values from -6 to 6
- cotangent: bfloat16 [4096, 4096], P(('dp', 'tensor')), may hold values from -6 to 6
- w_down: bfloat16 [16, 128, 128, 128], P('tensor', 'dp'), may hold values from -0.125 to 0.125
- block_hidden: int32 [16, 128], P('tensor'), may hold values from 0 to 6, as said below
- block_feat: int32 [16, 128], P('tensor'), may hold values from 0 to 31, as said below
- kept_counts: int32 [16], P('tensor'), may hold values from 64 to 128, as said below
Outputs:
- grad_gate: bfloat16 [4096, 14336], P('dp', 'tensor')
- grad_up: bfloat16 [4096, 14336], P('dp', 'tensor')
- grad_down: bfloat16 [16, 128, 128, 128], P('tensor', 'dp')
The draws below stay inside these ranges and needn't reach their ends.
Inputs may be any that keep to these rules, and one draw needn't show every extreme that they name: `block_hidden`: within one shard the 128 slots name distinct pairs of hidden block and feature block; slots past the shard's count are filled with further distinct pairs. `block_feat`: same pairs as block_hidden. `kept_counts`: some shard keeps all 128 slots in every draw.
All inputs are finite; a program needn't handle non-finite values.
Results may differ from the reference program's by a relative error of at most 0.023.
Values may be sent and summed in bfloat16 or wider, within the bound.
A program may use at most 64 MiB of HBM per device.

```python
import jax
import jax.numpy as jnp
from jax import lax

D = 4096
FF = 14336
BLOCK = 128
MAXB = 128
TOK = 128
TOKENS = 4096
FB = 7
DB = 32
N_DP = 32
N_TENSOR = 16


def block_pattern(key):
    keys = jax.random.split(key, N_TENSOR)
    picks = jax.vmap(lambda one: jax.random.permutation(one, FB * DB)[:MAXB])(keys)
    return picks.astype(jnp.int32)


def draw_block_hidden(key, part):
    return block_pattern(key) // DB


def draw_block_feat(key, part):
    return block_pattern(key) % DB


def draw_kept_counts(key, part):
    key = jax.random.fold_in(key, 7)
    count_key, busy_key = jax.random.split(key)
    counts = jax.random.randint(count_key, (N_TENSOR,), MAXB // 2, MAXB + 1)
    busiest = jax.random.randint(busy_key, (), 0, N_TENSOR)
    shards = jnp.arange(N_TENSOR, dtype=jnp.int32)
    return jnp.where(shards == busiest, MAXB, counts).astype(jnp.int32)


def block_levels(rng, dims, cuts, least, high):
    factor_of = 1.0
    for dim, shards_of in cuts:
        heights = jax.random.uniform(jax.random.fold_in(jax.random.fold_in(rng, 6), dim), (shards_of,), jnp.float32, least / len(cuts), high / len(cuts))
        factor_of = factor_of * jnp.repeat(jnp.exp(heights), dims[dim] // shards_of).reshape((-1,) + (1,) * (len(dims) - 1 - dim))
    return factor_of


def noise(stream_key, shape, deviation, bound, cuts=(), kind=jnp.bfloat16):
    values = jax.random.normal(stream_key, shape, jnp.float32) * deviation
    if len(cuts) > 0:
        values = block_levels(stream_key, shape, cuts, -0.22, 0.18) * values
    return jnp.clip(values, min=-bound, max=bound).astype(kind)


def setup_inputs(seed: int = 0) -> dict:
    streams_of = jax.random.split(jax.random.key(seed), 8)
    return {
        "gate_in": noise(streams_of[0], (TOKENS, FF), 1.5, 8.0, ((0, 32), (1, 16))),
        "up_in": noise(streams_of[1], (TOKENS, FF), 1.0, 6.0, ((0, 32), (1, 16))),
        "cotangent": noise(streams_of[2], (TOKENS, D), 1.0, 6.0, ((0, 512),)),
        "w_down": noise(streams_of[3], (N_TENSOR, MAXB, BLOCK, BLOCK), (D // 2) ** -0.5, 0.125, ((0, 16), (1, 32))),
        "block_hidden": draw_block_hidden(jax.random.fold_in(streams_of[7], 71), 0),
        "block_feat": draw_block_feat(jax.random.fold_in(streams_of[7], 71), 0),
        "kept_counts": draw_kept_counts(jax.random.fold_in(streams_of[7], 71), 0),
    }


def reference(gate_in, up_in, cotangent, w_down, block_hidden, block_feat, kept_counts):
    gate_f = gate_in.astype(jnp.float32)
    up_f = up_in.astype(jnp.float32)
    sigma = jax.nn.sigmoid(gate_f)
    active = gate_f * sigma
    hidden = (active * up_f).astype(jnp.bfloat16)
    hidden_parts = jnp.moveaxis(hidden.reshape(N_DP, TOK, N_TENSOR, FB, BLOCK), 2, 0)
    feature_parts = cotangent.reshape(N_DP, TOK, DB, BLOCK)
    slot_numbers = jnp.arange(MAXB, dtype=jnp.int32)

    def shard_pass(items):
        shard_hidden, shard_weights, hidden_ids, feature_ids, count = items

        def slot_step(accum, inner):
            weight, hid, feat, slot = inner
            live = (slot < count).astype(jnp.float32)
            picked = jnp.take(feature_parts, feat, axis=2).astype(jnp.float32)
            contrib = jnp.einsum("rtf,hf->rth", picked, weight.astype(jnp.float32)) * live
            accum = accum.at[:, :, hid].add(contrib)
            chosen = jnp.take(shard_hidden, hid, axis=2).astype(jnp.float32)
            partial_grad = jnp.einsum("rth,rtf->rhf", chosen, picked).astype(jnp.bfloat16)
            partial_grad = lax.optimization_barrier(partial_grad).astype(jnp.float32)
            summed = (jnp.sum(partial_grad, axis=0) * live).astype(jnp.bfloat16)
            return accum, summed

        start = jnp.zeros((N_DP, TOK, FB, BLOCK), jnp.float32)
        return lax.scan(slot_step, start, (shard_weights, hidden_ids, feature_ids, slot_numbers))

    grad_parts, grad_down = lax.map(shard_pass, (hidden_parts, w_down, block_hidden, block_feat, kept_counts))
    grad_hidden = jnp.moveaxis(grad_parts, 0, 2).reshape(TOKENS, FF)
    grad_gate = (grad_hidden * up_f * sigma * (1.0 + gate_f * (1.0 - sigma))).astype(jnp.bfloat16)
    grad_up = (grad_hidden * active).astype(jnp.bfloat16)
    return grad_gate, grad_up, grad_down
```

```python
import jax
import jax.numpy as jnp
from jax import lax
from jax.experimental import pallas as pl
from jax.experimental.pallas import tpu as pltpu
from jax.sharding import PartitionSpec as P

MESH = pl.DeviceIdType.MESH
F32 = jnp.float32
BF16 = jnp.bfloat16


def kernel(
    gate, up, cot, w, hid_ids, feat_ids, count,
    gg, gu, gd,
    raw, feats, hid_t, weights, spread, total, other,
    prod, s1, r1, s2, r2, part, t1, u1, t2, u2,
    send_sems, recv_sems,
):
    dp, tn = lax.axis_index("dp"), lax.axis_index("tensor")
    zh, y, c = dp // 8, (dp // 2) % 4, dp % 2
    x, zl = tn // 4, tn % 4

    def dev(dz=0, dy=0, other_core=False, dx=0, dl=0):
        core = 1 - c if other_core else c
        return (
            ((zh + dz) % 4) * 8 + ((y + dy) % 4) * 2 + core,
            ((x + dx) % 4) * 4 + (zl + dl) % 4,
        )

    sib = dev(other_core=True)
    yd = {1: dev(dy=1), -1: dev(dy=3)}
    zd = {1: dev(dz=1), -1: dev(dz=3)}
    xd = {1: dev(dx=1), -1: dev(dx=3)}
    ld = {k: dev(dl=k) for k in (1, 2, 3)}

    names = {}
    sent = []

    def number(name):
        return names.setdefault(name, len(names))

    def send(name, src, dst, to):
        i = number(name)
        copy = pltpu.make_async_remote_copy(
            src_ref=src, dst_ref=dst, send_sem=send_sems.at[i], recv_sem=recv_sems.at[i],
            device_id=to, device_id_type=MESH,
        )
        copy.start()
        sent.append(copy)

    def arrive(name, dst):
        i = number(name)
        pltpu.make_async_remote_copy(
            src_ref=dst, dst_ref=dst, send_sem=send_sems.at[i], recv_sem=recv_sems.at[i],
            device_id=sib, device_id_type=MESH,
        ).wait_recv()

    barrier = pltpu.get_barrier_semaphore()
    partners = [sib, *yd.values(), *zd.values(), *xd.values(), *ld.values()]
    for partner in partners:
        pl.semaphore_signal(barrier, inc=1, device_id=partner, device_id_type=MESH)

    weights[zh * 4 + y] = w[0]
    for fp in range(16):
        low = cot[:, fp * 128 : (fp + 1) * 128].astype(F32)
        high = cot[:, (fp + 16) * 128 : (fp + 17) * 128].astype(F32)
        raw[c, tn, fp] = jnp.concatenate([low, high], axis=0).astype(BF16)

    pl.semaphore_wait(barrier, len(partners))

    def cot_block(dx, k):
        return raw.at[c, ((x + dx) % 4) * 4 + (zl - k + 4) % 4]

    def cot_half(dx, k, half):
        return raw.at[c, ((x + dx) % 4) * 4 + (zl - k + 4) % 4, pl.ds(half * 8, 8)]

    def cot_sib(dx, k):
        return raw.at[1 - c, ((x + dx) % 4) * 4 + (zl - k + 4) % 4]

    def w_half(dz, dy, half):
        return weights.at[((zh + dz) % 4) * 4 + (y + dy) % 4, pl.ds(half * 2, 2)]

    def cot_out(k):
        own = cot_block(0, k)
        send(("ax", 1, k), own, own, xd[1])
        send(("ax", -1, k), own, own, xd[-1])
        send(("as", 0, k), own, own, sib)

    def w_out(dz, order=((1, 0), (-1, 1), (1, 1), (-1, 0))):
        for way, half in order:
            block = w_half(dz, 0, half)
            send(("by", way, dz, half), block, block, yd[way])

    def w_out_half(dz, half):
        block = w_half(dz, 0, half)
        for way in (1, -1):
            send(("by", way, dz, half), block, block, yd[way])

    def w_in(way, dz, half):
        block = w_half(dz, -way % 4, half)
        arrive(("by", way, dz, half), block)
        if (way, half) in ((1, 0), (-1, 1)):
            send(("bf", way, dz), block, block, yd[way])

    def w_in_forwards(dz):
        w_in(1, dz, 0)
        w_in(-1, dz, 1)

    def w_in_rest(dz):
        w_in(1, dz, 1)
        w_in(-1, dz, 0)
        arrive(("bf", 1, dz), w_half(dz, 2, 0))
        arrive(("bf", -1, dz), w_half(dz, 2, 1))

    own = cot_block(0, 0)
    for k in (1, 2, 3):
        send(("al", k), own, own, ld[k])
    cot_out(0)
    for way, half in ((1, 0), (-1, 1), (1, 1), (-1, 0)):
        block = w_half(0, 0, half)
        send(("bz", way, half), block, block, zd[way])
    w_out(0)

    for j in range(7):
        cols = slice(j * 128, (j + 1) * 128)
        g = gate[:, cols].astype(F32)
        active = g * (1.0 / (1.0 + jnp.exp(-g)))
        hidden = (active * up[:, cols].astype(F32)).astype(BF16)
        hid_t[c, j] = hidden.astype(F32).T.astype(BF16)
    send("hid", hid_t.at[c], hid_t.at[c], sib)

    def cot_in_lo(k):
        arrive(("al", k), cot_block(0, k))
        cot_out(k)

    def cot_in_x(k):
        for way, half in ((1, 0), (-1, 1)):
            arrive(("ax", way, k), cot_block(-way, k))
            piece = cot_half(-way, k, half)
            send(("af", way, k), piece, piece, xd[way])
            block = cot_block(-way, k)
            send(("as", -way, k), block, block, sib)

    def cot_in_far(k):
        arrive(("af", 1, k), cot_half(2, k, 0))
        arrive(("af", -1, k), cot_half(2, k, 1))
        block = cot_block(2, k)
        send(("as", 2, k), block, block, sib)

    def wz_in(way, half):
        block = w_half(-way, 0, half)
        arrive(("bz", way, half), block)
        if (way, half) in ((1, 0), (-1, 1)):
            send(("bzf", way), block, block, zd[way])
        w_out_half(-way, half)

    for k in (1, 2, 3):
        cot_in_lo(k)
    cot_in_x(0)
    w_in_forwards(0)
    cot_in_x(1)
    cot_in_x(2)
    cot_in_far(0)
    cot_in_x(3)
    wz_in(1, 0)
    wz_in(-1, 1)
    cot_in_far(1)
    cot_in_far(2)
    cot_in_far(3)

    for k in range(4):
        for dx in (0, 1, -1, 2):
            arrive(("as", dx, k), cot_sib(dx, k))
    arrive("hid", hid_t.at[1 - c])

    def repack(i, carry):
        core, pair = i // 8, i % 8
        first = raw[core, 2 * pair].astype(F32)
        second = raw[core, 2 * pair + 1].astype(F32)
        feats[0:16, i] = jnp.concatenate([first[:, :8], second[:, :8]], axis=1).astype(BF16)
        feats[16:32, i] = jnp.concatenate([first[:, 8:], second[:, 8:]], axis=1).astype(BF16)
        return carry

    lax.fori_loop(0, 16, repack, 0)

    def products(dz):
        def place(dy, carry):
            base = ((((zh + dz) % 4) * 4 + (y + dy) % 4) * 2 + c) * 4
            for q in range(4):
                hid = hid_ids[0, base + q]
                feat = feat_ids[0, base + q]
                left = jnp.concatenate([hid_t[0, hid], hid_t[1, hid]], axis=1)
                right = feats[feat].reshape(256, 128)
                prod[dz, dy, q] = jnp.dot(left, right, preferred_element_type=F32)
            return carry

        lax.fori_loop(0, 4, place, 0)

    def c1(dz):
        products(dz)
        for half, way in ((0, 1), (1, -1)):
            s1[dz, half] = prod[dz, 2, 2 * half : 2 * half + 2].astype(BF16)
            send(("c1", dz, half), s1.at[dz, half], r1.at[dz, half], yd[way])

    def c2(dz):
        for half, way, dy in ((0, 1, 1), (1, -1, 3)):
            rest = 1 - half
            s2[dz, half, 2 * rest : 2 * rest + 2] = prod[dz, dy, 2 * rest : 2 * rest + 2].astype(BF16)
            arrive(("c1", dz, half), r1.at[dz, half])
            s2[dz, half, 2 * half : 2 * half + 2] = (
                prod[dz, dy, 2 * half : 2 * half + 2] + r1[dz, half].astype(F32)
            ).astype(BF16)
            send(("c2", dz, half), s2.at[dz, half], r2.at[dz, half], yd[way])

    def c3(dz):
        arrive(("c2", dz, 0), r2.at[dz, 0])
        arrive(("c2", dz, 1), r2.at[dz, 1])
        part[dz] = prod[dz, 0] + r2[dz, 0].astype(F32) + r2[dz, 1].astype(F32)

    def d1():
        for half, way in ((0, 1), (1, -1)):
            t1[half] = part[2, 2 * half : 2 * half + 2].astype(BF16)
            send(("d1", half), t1.at[half], u1.at[half], zd[way])

    def d2():
        for half, way, dz in ((0, 1, 1), (1, -1, 3)):
            rest = 1 - half
            t2[half, 2 * rest : 2 * rest + 2] = part[dz, 2 * rest : 2 * rest + 2].astype(BF16)
            arrive(("d1", half), u1.at[half])
            t2[half, 2 * half : 2 * half + 2] = (
                part[dz, 2 * half : 2 * half + 2] + u1[half].astype(F32)
            ).astype(BF16)
            send(("d2", half), t2.at[half], u2.at[half], zd[way])

    c1(2)
    wz_in(1, 1)
    wz_in(-1, 0)
    c1(1)
    c2(2)
    c1(3)
    c2(1)
    c3(2)
    d1()
    c1(0)
    c2(3)
    c3(1)
    w_in_rest(0)
    w_in_forwards(1)
    w_in_forwards(-1)
    c2(0)
    c3(3)
    d2()
    c3(0)
    for way, half in ((1, 0), (-1, 1)):
        arrive(("bzf", way), w_half(2, 0, half))
        w_out_half(2, half)
    w_in_rest(1)
    w_in_rest(-1)
    w_in_forwards(2)
    w_in_rest(2)

    kept = count[0]
    total[...] = jnp.zeros_like(total)

    def accumulate(i, carry):
        base = (i * 2 + c) * 4
        picked = []
        for q in range(4):
            hid = jnp.where(base + q < kept, hid_ids[0, base + q], -1)
            picked.append(feats[feat_ids[0, base + q]].reshape(256, 128))
            block = weights[i, q]
            for j in range(7):
                spread[j * 128 : (j + 1) * 128, q * 128 : (q + 1) * 128] = jnp.where(
                    hid == j, block, jnp.zeros_like(block)
                )
        total[...] += lax.dot_general(
            jnp.concatenate(picked, axis=1), spread[...], (((1,), (1,)), ((), ())),
            preferred_element_type=F32,
        )
        return carry

    lax.fori_loop(0, 16, accumulate, 0)

    send("gh", total.at[pl.ds(pl.multiple_of((1 - c) * 128, 128), 128)], other, sib)

    arrive(("d2", 0), u2.at[0])
    arrive(("d2", 1), u2.at[1])
    for q in range(4):
        mine = part[0, q] + u2[0, q].astype(F32) + u2[1, q].astype(F32)
        live = jnp.where(dp * 4 + q < kept, 1.0, 0.0)
        gd[0, q] = (mine * live).astype(BF16)

    arrive("gh", other)
    for j in range(7):
        cols = slice(j * 128, (j + 1) * 128)
        grad = total[pl.ds(pl.multiple_of(c * 128, 128), 128), cols] + other[:, cols]
        g = gate[:, cols].astype(F32)
        u = up[:, cols].astype(F32)
        sigma = 1.0 / (1.0 + jnp.exp(-g))
        gg[:, cols] = (grad * u * sigma * (1.0 + g * (1.0 - sigma))).astype(BF16)
        gu[:, cols] = (grad * (g * sigma)).astype(BF16)

    for copy in sent:
        copy.wait_send()
    assert len(names) <= send_sems.shape[0]


def per_device(gate_in, up_in, cotangent, w_down, block_hidden, block_feat, kept_counts):
    vmem = pl.BlockSpec(memory_space=pltpu.VMEM)
    smem = pl.BlockSpec(memory_space=pltpu.SMEM)
    copies = 112
    return pl.pallas_call(
        kernel,
        out_shape=(
            jax.ShapeDtypeStruct(gate_in.shape, BF16),
            jax.ShapeDtypeStruct(up_in.shape, BF16),
            jax.ShapeDtypeStruct(w_down.shape, BF16),
        ),
        in_specs=[vmem, vmem, vmem, vmem, smem, smem, smem],
        out_specs=(vmem, vmem, vmem),
        scratch_shapes=[
            pltpu.VMEM((2, 16, 16, 16, 128), BF16),
            pltpu.VMEM((32, 16, 16, 128), BF16),
            pltpu.VMEM((2, 7, 128, 128), BF16),
            pltpu.VMEM((16, 4, 128, 128), BF16),
            pltpu.VMEM((896, 512), BF16),
            pltpu.VMEM((256, 896), F32),
            pltpu.VMEM((128, 896), F32),
            pltpu.VMEM((4, 4, 4, 128, 128), F32),
            pltpu.VMEM((4, 2, 2, 128, 128), BF16),
            pltpu.VMEM((4, 2, 2, 128, 128), BF16),
            pltpu.VMEM((4, 2, 4, 128, 128), BF16),
            pltpu.VMEM((4, 2, 4, 128, 128), BF16),
            pltpu.VMEM((4, 4, 128, 128), F32),
            pltpu.VMEM((2, 2, 128, 128), BF16),
            pltpu.VMEM((2, 2, 128, 128), BF16),
            pltpu.VMEM((2, 4, 128, 128), BF16),
            pltpu.VMEM((2, 4, 128, 128), BF16),
            pltpu.SemaphoreType.DMA((copies,)),
            pltpu.SemaphoreType.DMA((copies,)),
        ],
        compiler_params=pltpu.CompilerParams(
            collective_id=0, has_side_effects=True, vmem_limit_bytes=48 * 2**20
        ),
    )(gate_in, up_in, cotangent, w_down, block_hidden, block_feat, kept_counts)


def solution(mesh):
    return jax.shard_map(
        per_device,
        mesh=mesh,
        in_specs=(
            P("dp", "tensor"),
            P("dp", "tensor"),
            P(("dp", "tensor"), None),
            P("tensor", "dp", None, None),
            P("tensor", None),
            P("tensor", None),
            P("tensor"),
        ),
        out_specs=(P("dp", "tensor"), P("dp", "tensor"), P("tensor", "dp", None, None)),
        check_vma=False,
    )
```

```python
import jax
import jax.numpy as jnp
from jax import lax
from jax.experimental import pallas as pl
from jax.experimental.pallas import tpu as pltpu
from jax.sharding import PartitionSpec as P

MESH = pl.DeviceIdType.MESH
F32 = jnp.float32
BF16 = jnp.bfloat16


def kernel(
    gate_hbm, up_hbm, cot_hbm, w_hbm, hid_ids, feat_ids, count,
    gg, gu, gd,
    gate, up, cot, raw, feats, hid_t, weights, spread, total, other,
    prod, s1, r1, s2, r2, part, t1, u1, t2, u2,
    send_sems, recv_sems, load_sems,
):
    dp, tn = lax.axis_index("dp"), lax.axis_index("tensor")
    zh, y, c = dp // 8, (dp // 2) % 4, dp % 2
    x, zl = tn // 4, tn % 4

    def dev(dz=0, dy=0, other_core=False, dx=0, dl=0):
        core = 1 - c if other_core else c
        return (
            ((zh + dz) % 4) * 8 + ((y + dy) % 4) * 2 + core,
            ((x + dx) % 4) * 4 + (zl + dl) % 4,
        )

    sib = dev(other_core=True)
    yd = {1: dev(dy=1), -1: dev(dy=3)}
    zd = {1: dev(dz=1), -1: dev(dz=3)}
    xd = {1: dev(dx=1), -1: dev(dx=3)}
    ld = {k: dev(dl=k) for k in (1, 2, 3)}

    names = {}
    sent, started, arrived = [], [], []

    def number(name):
        return names.setdefault(name, len(names))

    def send(name, src, dst, to):
        i = number(name)
        copy = pltpu.make_async_remote_copy(
            src_ref=src, dst_ref=dst, send_sem=send_sems.at[i], recv_sem=recv_sems.at[i],
            device_id=to, device_id_type=MESH,
        )
        copy.start()
        sent.append(copy)
        started.append(name)

    def arrive(name, dst):
        i = number(name)
        assert name in started, name
        arrived.append(name)
        pltpu.make_async_remote_copy(
            src_ref=dst, dst_ref=dst, send_sem=send_sems.at[i], recv_sem=recv_sems.at[i],
            device_id=sib, device_id_type=MESH,
        ).wait_recv()

    barrier = pltpu.get_barrier_semaphore()
    partners = [sib, *yd.values(), *zd.values(), *xd.values(), *ld.values()]
    for partner in partners:
        pl.semaphore_signal(barrier, inc=1, device_id=partner, device_id_type=MESH)

    loads = [
        pltpu.make_async_copy(src, dst, load_sems.at[n])
        for n, (src, dst) in enumerate(
            ((cot_hbm, cot), (gate_hbm, gate), (up_hbm, up), (w_hbm.at[0], weights.at[zh * 4 + y]))
        )
    ]
    for load in loads:
        load.start()

    loads[0].wait()
    for fp in range(16):
        low = cot[:, fp * 128 : (fp + 1) * 128].astype(F32)
        high = cot[:, (fp + 16) * 128 : (fp + 17) * 128].astype(F32)
        raw[c, tn, fp] = jnp.concatenate([low, high], axis=0).astype(BF16)

    loads[1].wait()
    loads[2].wait()
    for j in range(7):
        cols = slice(j * 128, (j + 1) * 128)
        g = gate[:, cols].astype(F32)
        active = g * (1.0 / (1.0 + jnp.exp(-g)))
        hidden = (active * up[:, cols].astype(F32)).astype(BF16)
        hid_t[c, j] = hidden.astype(F32).T.astype(BF16)
    total[...] = jnp.zeros_like(total)
    loads[3].wait()

    pl.semaphore_wait(barrier, len(partners))

    def cot_block(dx, k):
        return raw.at[c, ((x + dx) % 4) * 4 + (zl - k + 4) % 4]

    def cot_half(dx, k, half):
        return raw.at[c, ((x + dx) % 4) * 4 + (zl - k + 4) % 4, pl.ds(half * 8, 8)]

    def cot_sib(dx, k):
        return raw.at[1 - c, ((x + dx) % 4) * 4 + (zl - k + 4) % 4]

    def w_half(dz, dy, half):
        return weights.at[((zh + dz) % 4) * 4 + (y + dy) % 4, pl.ds(half * 2, 2)]

    def cot_out(k):
        own = cot_block(0, k)
        send(("ax", 1, k), own, own, xd[1])
        send(("ax", -1, k), own, own, xd[-1])
        send(("as", 0, k), own, own, sib)

    def w_out(dz, order=((1, 0), (-1, 1), (1, 1), (-1, 0))):
        for way, half in order:
            block = w_half(dz, 0, half)
            send(("by", way, dz, half), block, block, yd[way])

    def w_out_half(dz, half):
        block = w_half(dz, 0, half)
        for way in (1, -1):
            send(("by", way, dz, half), block, block, yd[way])

    def w_in(way, dz, half):
        block = w_half(dz, -way % 4, half)
        arrive(("by", way, dz, half), block)
        if (way, half) in ((1, 0), (-1, 1)):
            send(("bf", way, dz), block, block, yd[way])

    def w_in_forwards(dz):
        w_in(1, dz, 0)
        w_in(-1, dz, 1)

    def w_in_rest(dz):
        w_in(1, dz, 1)
        w_in(-1, dz, 0)
        arrive(("bf", 1, dz), w_half(dz, 2, 0))
        arrive(("bf", -1, dz), w_half(dz, 2, 1))

    own = cot_block(0, 0)
    for k in (1, 2, 3):
        send(("al", k), own, own, ld[k])
    cot_out(0)
    for way, half in ((1, 0), (-1, 1), (1, 1), (-1, 0)):
        block = w_half(0, 0, half)
        send(("bz", way, half), block, block, zd[way])
    w_out(0)

    send("hid", hid_t.at[c], hid_t.at[c], sib)

    def cot_in_lo(k):
        arrive(("al", k), cot_block(0, k))
        cot_out(k)

    def cot_in_x(k):
        for way, half in ((1, 0), (-1, 1)):
            arrive(("ax", way, k), cot_block(-way, k))
            piece = cot_half(-way, k, half)
            send(("af", way, k), piece, piece, xd[way])
            block = cot_block(-way, k)
            send(("as", -way, k), block, block, sib)

    def cot_in_far(k):
        arrive(("af", 1, k), cot_half(2, k, 0))
        arrive(("af", -1, k), cot_half(2, k, 1))
        block = cot_block(2, k)
        send(("as", 2, k), block, block, sib)

    def wz_in(way, half):
        block = w_half(-way, 0, half)
        arrive(("bz", way, half), block)
        if (way, half) in ((1, 0), (-1, 1)):
            send(("bzf", way), block, block, zd[way])
        w_out_half(-way, half)

    def repack(dx):
        def step(i, carry):
            core, pair = i // 2, ((x + dx) % 4) * 2 + i % 2
            first = raw[core, 2 * pair].astype(F32)
            second = raw[core, 2 * pair + 1].astype(F32)
            at = core * 8 + pair
            feats[0:16, at] = jnp.concatenate([first[:, :8], second[:, :8]], axis=1).astype(BF16)
            feats[16:32, at] = jnp.concatenate([first[:, 8:], second[:, 8:]], axis=1).astype(BF16)
            return carry

        lax.fori_loop(0, 4, step, 0)

    def from_sib(dx, ks):
        for k in ks:
            arrive(("as", dx, k), cot_sib(dx, k))

    def products(dz):
        def place(dy, carry):
            base = ((((zh + dz) % 4) * 4 + (y + dy) % 4) * 2 + c) * 4
            for q in range(4):
                hid = hid_ids[0, base + q]
                feat = feat_ids[0, base + q]
                left = jnp.concatenate([hid_t[0, hid], hid_t[1, hid]], axis=1)
                right = feats[feat].reshape(256, 128)
                prod[dz, dy, q] = jnp.dot(left, right, preferred_element_type=F32)
            return carry

        lax.fori_loop(0, 4, place, 0)

    def pair(half):
        return slice(2 * half, 2 * half + 2)

    def piece(half):
        return pl.ds(2 * half, 2)

    def c1(dz):
        for half, way in ((0, 1), (1, -1)):
            s1[dz, half] = prod[dz, 2, pair(half)].astype(BF16)
            send(("c1", dz, half), s1.at[dz, half], r1.at[dz, half], yd[way])
        for half, way, dy in ((0, 1, 1), (1, -1, 3)):
            rest = 1 - half
            s2[dz, half, pair(rest)] = prod[dz, dy, pair(rest)].astype(BF16)
            send(("cp", dz, half), s2.at[dz, half, piece(rest)], r2.at[dz, half, piece(rest)], yd[way])

    def c2(dz):
        for half, way, dy in ((0, 1, 1), (1, -1, 3)):
            arrive(("c1", dz, half), r1.at[dz, half])
            s2[dz, half, pair(half)] = (
                prod[dz, dy, pair(half)] + r1[dz, half].astype(F32)
            ).astype(BF16)
            send(("cs", dz, half), s2.at[dz, half, piece(half)], r2.at[dz, half, piece(half)], yd[way])

    def c3(dz):
        for half in (0, 1):
            arrive(("cp", dz, half), r2.at[dz, half, piece(1 - half)])
        for half in (0, 1):
            arrive(("cs", dz, half), r2.at[dz, half, piece(half)])
        part[dz] = prod[dz, 0] + r2[dz, 0].astype(F32) + r2[dz, 1].astype(F32)

    def d1():
        for half, way in ((0, 1), (1, -1)):
            t1[half] = part[2, pair(half)].astype(BF16)
            send(("d1", half), t1.at[half], u1.at[half], zd[way])

    def d2_plain(half, way, dz):
        rest = 1 - half
        t2[half, pair(rest)] = part[dz, pair(rest)].astype(BF16)
        send(("dp", half), t2.at[half, piece(rest)], u2.at[half, piece(rest)], zd[way])

    def d2():
        for half, way, dz in ((0, 1, 1), (1, -1, 3)):
            arrive(("d1", half), u1.at[half])
            t2[half, pair(half)] = (part[dz, pair(half)] + u1[half].astype(F32)).astype(BF16)
            send(("ds", half), t2.at[half, piece(half)], u2.at[half, piece(half)], zd[way])

    kept = count[0]

    def accumulate(dz):
        def place(dy, carry):
            at = ((zh + dz) % 4) * 4 + (y + dy) % 4
            base = (at * 2 + c) * 4
            picked = []
            for q in range(4):
                hid = jnp.where(base + q < kept, hid_ids[0, base + q], -1)
                picked.append(feats[feat_ids[0, base + q]].reshape(256, 128))
                block = weights[at, q]
                for j in range(7):
                    spread[j * 128 : (j + 1) * 128, q * 128 : (q + 1) * 128] = jnp.where(
                        hid == j, block, jnp.zeros_like(block)
                    )
            total[...] += lax.dot_general(
                jnp.concatenate(picked, axis=1), spread[...], (((1,), (1,)), ((), ())),
                preferred_element_type=F32,
            )
            return carry

        lax.fori_loop(0, 4, place, 0)

    cot_in_lo(1)
    cot_in_lo(3)
    cot_in_x(1)
    cot_in_lo(2)
    cot_in_x(0)
    cot_in_x(3)
    cot_in_x(2)
    arrive("hid", hid_t.at[1 - c])
    w_in_forwards(0)
    from_sib(-1, (0, 1, 2, 3))
    repack(3)
    wz_in(1, 0)
    wz_in(-1, 1)
    from_sib(0, (0, 1, 2, 3))
    repack(0)
    cot_in_far(1)
    cot_in_far(3)
    cot_in_far(2)
    cot_in_far(0)
    from_sib(2, (0, 1, 2, 3))
    repack(2)
    from_sib(1, (0, 1, 2, 3))
    repack(1)
    w_in_rest(0)
    products(2)
    c1(2)
    products(1)
    c1(1)
    products(0)
    c2(2)
    products(3)
    c1(3)
    c3(2)
    d1()
    c2(1)
    c2(3)
    wz_in(1, 1)
    wz_in(-1, 0)
    accumulate(0)
    c3(3)
    c3(1)
    d2_plain(1, -1, 3)
    for way, half in ((1, 0), (-1, 1)):
        arrive(("bzf", way), w_half(2, 0, half))
        w_out_half(2, half)
    d2_plain(0, 1, 1)
    w_in_forwards(1)
    d2()
    w_in_forwards(-1)
    w_in_forwards(2)
    w_in_rest(1)
    c1(0)
    accumulate(1)
    w_in_rest(-1)
    accumulate(3)
    c2(0)
    w_in_rest(2)
    accumulate(2)
    c3(0)

    send("gh", total.at[pl.ds(pl.multiple_of((1 - c) * 128, 128), 128)], other, sib)

    for half in (0, 1):
        arrive(("dp", half), u2.at[half, piece(1 - half)])
        arrive(("ds", half), u2.at[half, piece(half)])
    for q in range(4):
        mine = part[0, q] + u2[0, q].astype(F32) + u2[1, q].astype(F32)
        live = jnp.where(dp * 4 + q < kept, 1.0, 0.0)
        gd[0, q] = (mine * live).astype(BF16)

    arrive("gh", other)
    for j in range(7):
        cols = slice(j * 128, (j + 1) * 128)
        grad = total[pl.ds(pl.multiple_of(c * 128, 128), 128), cols] + other[:, cols]
        g = gate[:, cols].astype(F32)
        u = up[:, cols].astype(F32)
        sigma = 1.0 / (1.0 + jnp.exp(-g))
        gg[:, cols] = (grad * u * sigma * (1.0 + g * (1.0 - sigma))).astype(BF16)
        gu[:, cols] = (grad * (g * sigma)).astype(BF16)

    for copy in sent:
        copy.wait_send()
    assert len(names) == len(started) == len(arrived) <= send_sems.shape[0]


def per_device(gate_in, up_in, cotangent, w_down, block_hidden, block_feat, kept_counts):
    vmem = pl.BlockSpec(memory_space=pltpu.VMEM)
    hbm = pl.BlockSpec(memory_space=pl.ANY)
    smem = pl.BlockSpec(memory_space=pltpu.SMEM)
    copies = 128
    return pl.pallas_call(
        kernel,
        out_shape=(
            jax.ShapeDtypeStruct(gate_in.shape, BF16),
            jax.ShapeDtypeStruct(up_in.shape, BF16),
            jax.ShapeDtypeStruct(w_down.shape, BF16),
        ),
        in_specs=[hbm, hbm, hbm, hbm, smem, smem, smem],
        out_specs=(vmem, vmem, vmem),
        scratch_shapes=[
            pltpu.VMEM(gate_in.shape, BF16),
            pltpu.VMEM(up_in.shape, BF16),
            pltpu.VMEM(cotangent.shape, BF16),
            pltpu.VMEM((2, 16, 16, 16, 128), BF16),
            pltpu.VMEM((32, 16, 16, 128), BF16),
            pltpu.VMEM((2, 7, 128, 128), BF16),
            pltpu.VMEM((16, 4, 128, 128), BF16),
            pltpu.VMEM((896, 512), BF16),
            pltpu.VMEM((256, 896), F32),
            pltpu.VMEM((128, 896), F32),
            pltpu.VMEM((4, 4, 4, 128, 128), F32),
            pltpu.VMEM((4, 2, 2, 128, 128), BF16),
            pltpu.VMEM((4, 2, 2, 128, 128), BF16),
            pltpu.VMEM((4, 2, 4, 128, 128), BF16),
            pltpu.VMEM((4, 2, 4, 128, 128), BF16),
            pltpu.VMEM((4, 4, 128, 128), F32),
            pltpu.VMEM((2, 2, 128, 128), BF16),
            pltpu.VMEM((2, 2, 128, 128), BF16),
            pltpu.VMEM((2, 4, 128, 128), BF16),
            pltpu.VMEM((2, 4, 128, 128), BF16),
            pltpu.SemaphoreType.DMA((copies,)),
            pltpu.SemaphoreType.DMA((copies,)),
            pltpu.SemaphoreType.DMA((4,)),
        ],
        compiler_params=pltpu.CompilerParams(
            collective_id=0, has_side_effects=True, vmem_limit_bytes=60 * 2**20
        ),
    )(gate_in, up_in, cotangent, w_down, block_hidden, block_feat, kept_counts)


def solution(mesh):
    return jax.shard_map(
        per_device,
        mesh=mesh,
        in_specs=(
            P("dp", "tensor"),
            P("dp", "tensor"),
            P(("dp", "tensor"), None),
            P("tensor", "dp", None, None),
            P("tensor", None),
            P("tensor", None),
            P("tensor"),
        ),
        out_specs=(P("dp", "tensor"), P("dp", "tensor"), P("tensor", "dp", None, None)),
        check_vma=False,
    )
```

```python
import jax
import jax.numpy as jnp
from jax import lax
from jax.experimental import pallas as pl
from jax.experimental.pallas import tpu as pltpu
from jax.sharding import PartitionSpec as P

MESH = pl.DeviceIdType.MESH
F32 = jnp.float32
BF16 = jnp.bfloat16
FORWARD = ((1, 0), (-1, 1))
OTHER = ((1, 1), (-1, 0))
DIRECT = (3,)


def kernel(
    gate_hbm, up_hbm, cot_hbm, w_hbm, hid_ids, feat_ids, count,
    grad, down,
    gate, up, cot, raw, feats, hid_t, weights, spread, total, other,
    prod, s1, r1, s2, r2, part, t1, u1, t2, u2,
    send_sems, recv_sems, load_sems,
):
    dp, tn = lax.axis_index("dp"), lax.axis_index("tensor")
    zh, y, c = dp // 8, (dp // 2) % 4, dp % 2
    x, zl = tn // 4, tn % 4

    def dev(dz=0, dy=0, other_core=False, dx=0, dl=0):
        core = 1 - c if other_core else c
        return (
            ((zh + dz) % 4) * 8 + ((y + dy) % 4) * 2 + core,
            ((x + dx) % 4) * 4 + (zl + dl) % 4,
        )

    sib = dev(other_core=True)
    yd = {1: dev(dy=1), -1: dev(dy=3)}
    zd = {1: dev(dz=1), -1: dev(dz=3)}
    xd = {1: dev(dx=1), -1: dev(dx=3), 2: dev(dx=2)}
    ld = {k: dev(dl=k) for k in (1, 2, 3)}

    names = {}
    sent, started, arrived = [], [], []

    def number(name):
        return names.setdefault(name, len(names))

    def send(name, src, dst, to):
        i = number(name)
        copy = pltpu.make_async_remote_copy(
            src_ref=src, dst_ref=dst, send_sem=send_sems.at[i], recv_sem=recv_sems.at[i],
            device_id=to, device_id_type=MESH,
        )
        copy.start()
        sent.append(copy)
        started.append(name)

    def arrive(name, dst):
        i = number(name)
        assert name in started, name
        arrived.append(name)
        pltpu.make_async_remote_copy(
            src_ref=dst, dst_ref=dst, send_sem=send_sems.at[i], recv_sem=recv_sems.at[i],
            device_id=sib, device_id_type=MESH,
        ).wait_recv()

    barrier = pltpu.get_barrier_semaphore()
    partners = [sib, *yd.values(), *zd.values(), *xd.values(), *ld.values()]
    for partner in partners:
        pl.semaphore_signal(barrier, inc=1, device_id=partner, device_id_type=MESH)

    loads = [
        pltpu.make_async_copy(src, dst, load_sems.at[n])
        for n, (src, dst) in enumerate(
            ((cot_hbm, cot), (gate_hbm, gate), (up_hbm, up), (w_hbm.at[0], weights.at[zh * 4 + y]))
        )
    ]
    for load in loads:
        load.start()

    loads[0].wait()
    for fp in range(16):
        low = cot[:, fp * 128 : (fp + 1) * 128].astype(F32)
        high = cot[:, (fp + 16) * 128 : (fp + 17) * 128].astype(F32)
        raw[c, tn, fp] = jnp.concatenate([low, high], axis=0).astype(BF16)

    loads[1].wait()
    loads[2].wait()
    for j in range(7):
        cols = slice(j * 128, (j + 1) * 128)
        g = gate[:, cols].astype(F32)
        active = g * (1.0 / (1.0 + jnp.exp(-g)))
        hidden = (active * up[:, cols].astype(F32)).astype(BF16)
        hid_t[c, j] = hidden.astype(F32).T.astype(BF16)
    total[...] = jnp.zeros_like(total)
    loads[3].wait()

    pl.semaphore_wait(barrier, len(partners))

    def cot_block(dx, k):
        return raw.at[c, ((x + dx) % 4) * 4 + (zl - k + 4) % 4]

    def cot_half(dx, k, half):
        return raw.at[c, ((x + dx) % 4) * 4 + (zl - k + 4) % 4, pl.ds(half * 8, 8)]

    def cot_sib(dx, k):
        return raw.at[1 - c, ((x + dx) % 4) * 4 + (zl - k + 4) % 4]

    def w_half(dz, dy, half):
        return weights.at[((zh + dz) % 4) * 4 + (y + dy) % 4, pl.ds(half * 2, 2)]

    def cot_out(k):
        own = cot_block(0, k)
        send(("ax", 1, k), own, own, xd[1])
        send(("ax", -1, k), own, own, xd[-1])
        send(("as", 0, k), own, own, sib)
        if k in DIRECT:
            send(("ax", 2, k), own, own, xd[2])

    def w_out_y(pieces):
        for way, half in pieces:
            block = w_half(0, 0, half)
            send(("by", way, 0, half), block, block, yd[way])

    def w_out_z(pieces):
        for way, half in pieces:
            block = w_half(0, 0, half)
            send(("bz", way, half), block, block, zd[way])

    def w_out_half(dz, half):
        block = w_half(dz, 0, half)
        for way in (1, -1):
            send(("by", way, dz, half), block, block, yd[way])

    def w_in(way, dz, half):
        block = w_half(dz, -way % 4, half)
        arrive(("by", way, dz, half), block)
        if (way, half) in FORWARD:
            send(("bf", way, dz), block, block, yd[way])

    def w_in_far(dz, way):
        arrive(("bf", way, dz), w_half(dz, 2, 0 if way == 1 else 1))

    def wz_in(way, half):
        block = w_half(-way, 0, half)
        arrive(("bz", way, half), block)
        if (way, half) in FORWARD:
            send(("bzf", way), block, block, zd[way])

    def wz_in_far(way):
        arrive(("bzf", way), w_half(2, 0, 0 if way == 1 else 1))

    own = cot_block(0, 0)
    for k in (1, 2, 3):
        send(("al", k), own, own, ld[k])
    cot_out(0)
    send("hid", hid_t.at[c], hid_t.at[c], sib)

    def cot_in_lo(k):
        arrive(("al", k), cot_block(0, k))
        cot_out(k)

    def cot_in_x(k, way):
        block = cot_block(-way, k)
        arrive(("ax", way, k), block)
        if k not in DIRECT:
            part_of = cot_half(-way, k, 0 if way == 1 else 1)
            send(("af", way, k), part_of, part_of, xd[way])
        send(("as", -way, k), block, block, sib)

    def cot_in_far(k):
        block = cot_block(2, k)
        if k in DIRECT:
            arrive(("ax", 2, k), block)
        else:
            arrive(("af", 1, k), cot_half(2, k, 0))
            arrive(("af", -1, k), cot_half(2, k, 1))
        send(("as", 2, k), block, block, sib)

    def repack(dx):
        def step(i, carry):
            core, pair = i // 2, ((x + dx) % 4) * 2 + i % 2
            first = raw[core, 2 * pair].astype(F32)
            second = raw[core, 2 * pair + 1].astype(F32)
            at = core * 8 + pair
            feats[0:16, at] = jnp.concatenate([first[:, :8], second[:, :8]], axis=1).astype(BF16)
            feats[16:32, at] = jnp.concatenate([first[:, 8:], second[:, 8:]], axis=1).astype(BF16)
            return carry

        lax.fori_loop(0, 4, step, 0)

    def from_sib(dx, ks):
        for k in ks:
            arrive(("as", dx, k), cot_sib(dx, k))

    def products(dz):
        def place(dy, carry):
            base = ((((zh + dz) % 4) * 4 + (y + dy) % 4) * 2 + c) * 4
            for q in range(4):
                hid = hid_ids[0, base + q]
                feat = feat_ids[0, base + q]
                left = jnp.concatenate([hid_t[0, hid], hid_t[1, hid]], axis=1)
                right = feats[feat].reshape(256, 128)
                prod[dz, dy, q] = jnp.dot(left, right, preferred_element_type=F32)
            return carry

        lax.fori_loop(0, 4, place, 0)

    def pair(half):
        return slice(2 * half, 2 * half + 2)

    def piece(half):
        return pl.ds(2 * half, 2)

    def c1(dz):
        for half, way in ((0, 1), (1, -1)):
            s1[dz, half] = prod[dz, 2, pair(half)].astype(BF16)
            send(("c1", dz, half), s1.at[dz, half], r1.at[dz, half], yd[way])

    def cp(dz):
        for half, way, dy in ((0, 1, 1), (1, -1, 3)):
            rest = 1 - half
            s2[dz, half, pair(rest)] = prod[dz, dy, pair(rest)].astype(BF16)
            send(("cp", dz, half), s2.at[dz, half, piece(rest)], r2.at[dz, half, piece(rest)], yd[way])

    def c2(dz, half):
        way, dy = ((1, 1), (-1, 3))[half]
        arrive(("c1", dz, half), r1.at[dz, half])
        s2[dz, half, pair(half)] = (prod[dz, dy, pair(half)] + r1[dz, half].astype(F32)).astype(BF16)
        send(("cs", dz, half), s2.at[dz, half, piece(half)], r2.at[dz, half, piece(half)], yd[way])

    def c3(dz, half):
        other_half = 1 - half
        arrive(("cp", dz, other_half), r2.at[dz, other_half, piece(half)])
        arrive(("cs", dz, half), r2.at[dz, half, piece(half)])
        rows = pair(half)
        part[dz, rows] = prod[dz, 0, rows] + r2[dz, 0, rows].astype(F32) + r2[dz, 1, rows].astype(F32)

    def d1(half):
        t1[half] = part[2, pair(half)].astype(BF16)
        send(("d1", half), t1.at[half], u1.at[half], zd[(1, -1)[half]])

    def d2_plain(dz):
        half, way = {1: (0, 1), 3: (1, -1)}[dz]
        rest = 1 - half
        t2[half, pair(rest)] = part[dz, pair(rest)].astype(BF16)
        send(("dp", half), t2.at[half, piece(rest)], u2.at[half, piece(rest)], zd[way])

    def d2(half):
        way, dz = ((1, 1), (-1, 3))[half]
        arrive(("d1", half), u1.at[half])
        t2[half, pair(half)] = (part[dz, pair(half)] + u1[half].astype(F32)).astype(BF16)
        send(("ds", half), t2.at[half, piece(half)], u2.at[half, piece(half)], zd[way])

    kept = count[0]

    def accumulate(dz, dy):
        at = ((zh + dz) % 4) * 4 + (y + dy) % 4
        base = (at * 2 + c) * 4
        picked = []
        for q in range(4):
            hid = jnp.where(base + q < kept, hid_ids[0, base + q], -1)
            picked.append(feats[feat_ids[0, base + q]].reshape(256, 128))
            block = weights[at, q]
            for j in range(7):
                spread[j * 128 : (j + 1) * 128, q * 128 : (q + 1) * 128] = jnp.where(
                    hid == j, block, jnp.zeros_like(block)
                )
        total[...] += lax.dot_general(
            jnp.concatenate(picked, axis=1), spread[...], (((1,), (1,)), ((), ())),
            preferred_element_type=F32,
        )

    def exchange():
        send("gh", total.at[pl.ds(pl.multiple_of((1 - c) * 128, 128), 128)], other, sib)

    def block_sums():
        for half in (0, 1):
            arrive(("dp", half), u2.at[half, piece(1 - half)])
            arrive(("ds", half), u2.at[half, piece(half)])
        for q in range(4):
            live = jnp.where(dp * 4 + q < kept, 1.0, 0.0)
            down[0, q] = (part[0, q] + u2[0, q].astype(F32) + u2[1, q].astype(F32)) * live

    def finish():
        arrive("gh", other)
        grad[...] = total[pl.ds(pl.multiple_of(c * 128, 128), 128), :] + other[...]

    cot_in_lo(1)
    w_out_y(FORWARD)
    w_out_z(FORWARD)
    w_out_y(OTHER)
    cot_in_lo(2)
    cot_in_lo(3)
    cot_in_x(1, 1)
    from_sib(0, (0, 1, 2, 3))
    repack(0)
    cot_in_x(1, -1)
    arrive("hid", hid_t.at[1 - c])
    w_in(1, 0, 0)
    cot_in_x(0, 1)
    cot_in_x(0, -1)
    cot_in_x(2, -1)
    cot_in_x(2, 1)
    cot_in_x(3, 1)
    w_in(1, 0, 1)
    w_out_z(OTHER)
    w_in(-1, 0, 1)
    w_in(-1, 0, 0)
    cot_in_x(3, -1)
    cot_in_far(3)
    wz_in(-1, 1)
    w_out_half(1, 1)
    wz_in(1, 0)
    from_sib(1, (0, 1, 2, 3))
    repack(1)
    cot_in_far(1)
    cot_in_far(0)
    cot_in_far(2)
    from_sib(-1, (0, 1, 2, 3))
    repack(3)
    w_out_half(-1, 0)
    from_sib(2, (0, 1, 2, 3))
    repack(2)
    w_in_far(0, -1)
    products(2)
    c1(2)
    products(3)
    products(1)
    c1(3)
    cp(2)
    c1(1)
    c2(2, 1)
    c2(2, 0)
    accumulate(0, 0)
    cp(1)
    c2(1, 1)
    c2(1, 0)
    wz_in(1, 1)
    c2(3, 1)
    c2(3, 0)
    cp(3)
    wz_in(-1, 0)
    c3(2, 0)
    d1(0)
    c3(2, 1)
    d1(1)
    wz_in_far(1)
    products(0)
    w_in(-1, 1, 1)
    w_in(1, 1, 1)
    w_in(1, -1, 0)
    w_out_half(-1, 1)
    accumulate(1, 0)
    accumulate(3, 0)
    w_in(-1, -1, 0)
    c3(1, 1)
    w_out_half(2, 0)
    wz_in_far(-1)
    c3(3, 0)
    w_out_half(2, 1)
    d2_plain(1)
    d2_plain(3)
    c3(3, 1)
    w_out_half(1, 0)
    accumulate(0, 3)
    w_in_far(0, 1)
    w_in(1, -1, 1)
    c1(0)
    w_in(1, 2, 0)
    accumulate(2, 0)
    c3(1, 0)
    d2(0)
    d2(1)
    accumulate(0, 2)
    w_in(-1, -1, 1)
    w_in(1, 1, 0)
    w_in(-1, 2, 1)
    accumulate(1, 3)
    accumulate(3, 1)
    w_in(-1, 1, 0)
    accumulate(0, 1)
    c2(0, 1)
    accumulate(3, 3)
    w_in_far(-1, 1)
    w_in(1, 2, 1)
    cp(0)
    w_in(-1, 2, 0)
    accumulate(2, 1)
    w_in_far(1, -1)
    accumulate(2, 3)
    w_in_far(2, 1)
    c2(0, 0)
    accumulate(1, 1)
    w_in_far(-1, -1)
    w_in_far(2, -1)
    accumulate(3, 2)
    accumulate(2, 2)
    w_in_far(1, 1)
    accumulate(1, 2)
    exchange()
    c3(0, 1)
    c3(0, 0)
    block_sums()
    finish()

    for copy in sent:
        copy.wait_send()
    assert len(names) == len(started) == len(arrived) <= send_sems.shape[0]


def per_device(gate_in, up_in, cotangent, w_down, block_hidden, block_feat, kept_counts):
    vmem = pl.BlockSpec(memory_space=pltpu.VMEM)
    hbm = pl.BlockSpec(memory_space=pl.ANY)
    smem = pl.BlockSpec(memory_space=pltpu.SMEM)
    copies = 128
    grad, down = pl.pallas_call(
        kernel,
        out_shape=(
            jax.ShapeDtypeStruct(gate_in.shape, F32),
            jax.ShapeDtypeStruct(w_down.shape, F32),
        ),
        in_specs=[hbm, hbm, hbm, hbm, smem, smem, smem],
        out_specs=(vmem, vmem),
        scratch_shapes=[
            pltpu.VMEM(gate_in.shape, BF16),
            pltpu.VMEM(up_in.shape, BF16),
            pltpu.VMEM(cotangent.shape, BF16),
            pltpu.VMEM((2, 16, 16, 16, 128), BF16),
            pltpu.VMEM((32, 16, 16, 128), BF16),
            pltpu.VMEM((2, 7, 128, 128), BF16),
            pltpu.VMEM((16, 4, 128, 128), BF16),
            pltpu.VMEM((896, 512), BF16),
            pltpu.VMEM((256, 896), F32),
            pltpu.VMEM((128, 896), F32),
            pltpu.VMEM((4, 4, 4, 128, 128), F32),
            pltpu.VMEM((4, 2, 2, 128, 128), BF16),
            pltpu.VMEM((4, 2, 2, 128, 128), BF16),
            pltpu.VMEM((4, 2, 4, 128, 128), BF16),
            pltpu.VMEM((4, 2, 4, 128, 128), BF16),
            pltpu.VMEM((4, 4, 128, 128), F32),
            pltpu.VMEM((2, 2, 128, 128), BF16),
            pltpu.VMEM((2, 2, 128, 128), BF16),
            pltpu.VMEM((2, 4, 128, 128), BF16),
            pltpu.VMEM((2, 4, 128, 128), BF16),
            pltpu.SemaphoreType.DMA((copies,)),
            pltpu.SemaphoreType.DMA((copies,)),
            pltpu.SemaphoreType.DMA((4,)),
        ],
        compiler_params=pltpu.CompilerParams(
            collective_id=0, has_side_effects=True, vmem_limit_bytes=60 * 2**20
        ),
    )(gate_in, up_in, cotangent, w_down, block_hidden, block_feat, kept_counts)
    g, u = gate_in.astype(F32), up_in.astype(F32)
    sigma = jax.nn.sigmoid(g)
    grad_gate = (grad * u * sigma * (1.0 + g * (1.0 - sigma))).astype(BF16)
    grad_up = (grad * (g * sigma)).astype(BF16)
    return grad_gate, grad_up, down.astype(BF16)


def solution(mesh):
    return jax.shard_map(
        per_device,
        mesh=mesh,
        in_specs=(
            P("dp", "tensor"),
            P("dp", "tensor"),
            P(("dp", "tensor"), None),
            P("tensor", "dp", None, None),
            P("tensor", None),
            P("tensor", None),
            P("tensor"),
        ),
        out_specs=(P("dp", "tensor"), P("dp", "tensor"), P("tensor", "dp", None, None)),
        check_vma=False,
    )
```

```python
import jax
import jax.numpy as jnp
from jax import lax
from jax.experimental import pallas as pl
from jax.experimental.pallas import tpu as pltpu
from jax.sharding import PartitionSpec as P

MESH = pl.DeviceIdType.MESH
F32 = jnp.float32
BF16 = jnp.bfloat16
FORWARD = ((1, 0), (-1, 1))
OTHER = ((1, 1), (-1, 0))
DIRECT = (3,)


def kernel(
    gate_hbm, up_hbm, cot_hbm, w_hbm, hid_ids, feat_ids, count,
    grad, down,
    gate, up, cot, raw, feats, hid_t, weights, spread, total, other,
    prod, s1, r1, s2, r2, part, t1, u1, t2, u2,
    send_sems, recv_sems, load_sems, ready, z_ready,
):
    dp, tn = lax.axis_index("dp"), lax.axis_index("tensor")
    zh, y, c = dp // 8, (dp // 2) % 4, dp % 2
    x, zl = tn // 4, tn % 4

    def dev(dz=0, dy=0, other_core=False, dx=0, dl=0):
        core = 1 - c if other_core else c
        return (
            ((zh + dz) % 4) * 8 + ((y + dy) % 4) * 2 + core,
            ((x + dx) % 4) * 4 + (zl + dl) % 4,
        )

    sib = dev(other_core=True)
    yd = {1: dev(dy=1), -1: dev(dy=3)}
    zd = {1: dev(dz=1), -1: dev(dz=3)}
    xd = {1: dev(dx=1), -1: dev(dx=3), 2: dev(dx=2)}
    ld = {k: dev(dl=k) for k in (1, 2, 3)}

    names = {}
    sent, started, arrived = [], [], []

    def number(name):
        return names.setdefault(name, len(names))

    def send(name, src, dst, to):
        i = number(name)
        copy = pltpu.make_async_remote_copy(
            src_ref=src, dst_ref=dst, send_sem=send_sems.at[i], recv_sem=recv_sems.at[i],
            device_id=to, device_id_type=MESH,
        )
        copy.start()
        sent.append(copy)
        started.append(name)

    def arrive(name, dst):
        i = number(name)
        assert name in started, name
        arrived.append(name)
        pltpu.make_async_remote_copy(
            src_ref=dst, dst_ref=dst, send_sem=send_sems.at[i], recv_sem=recv_sems.at[i],
            device_id=sib, device_id_type=MESH,
        ).wait_recv()

    barrier = pltpu.get_barrier_semaphore()
    near = [*yd.values(), *xd.values(), *ld.values()]

    def signal(sem, to):
        pl.semaphore_signal(sem, inc=1, device_id=to, device_id_type=MESH)

    @pl.when(c == 0)
    def _():
        for neighbour in near:
            signal(barrier, neighbour)

    @pl.when(c == 1)
    def _():
        signal(barrier, sib)

    loads = [
        pltpu.make_async_copy(src, dst, load_sems.at[n])
        for n, (src, dst) in enumerate(
            ((cot_hbm, cot), (gate_hbm, gate), (up_hbm, up), (w_hbm.at[0], weights.at[zh * 4 + y]))
        )
    ]
    for load in loads:
        load.start()

    loads[0].wait()
    for fp in range(16):
        low = cot[:, fp * 128 : (fp + 1) * 128].astype(F32)
        high = cot[:, (fp + 16) * 128 : (fp + 17) * 128].astype(F32)
        raw[c, tn, fp] = jnp.concatenate([low, high], axis=0).astype(BF16)

    loads[1].wait()
    loads[2].wait()
    for j in range(7):
        cols = slice(j * 128, (j + 1) * 128)
        g = gate[:, cols].astype(F32)
        active = g * (1.0 / (1.0 + jnp.exp(-g)))
        hidden = (active * up[:, cols].astype(F32)).astype(BF16)
        hid_t[c, j] = hidden.astype(F32).T.astype(BF16)
    total[...] = jnp.zeros_like(total)
    loads[3].wait()

    @pl.when(c == 0)
    def _():
        pl.semaphore_wait(barrier, len(near) + 1)
        for neighbour in near:
            signal(ready, neighbour)
        pl.semaphore_wait(ready, len(near))
        signal(ready, sib)

    @pl.when(c == 1)
    def _():
        pl.semaphore_wait(ready, 1)
        for partner in zd.values():
            signal(barrier, partner)

    def through_z():
        @pl.when(c == 1)
        def _():
            pl.semaphore_wait(barrier, 2)
            signal(z_ready, sib)

        @pl.when(c == 0)
        def _():
            pl.semaphore_wait(z_ready, 1)

    def cot_block(dx, k):
        return raw.at[c, ((x + dx) % 4) * 4 + (zl - k + 4) % 4]

    def cot_half(dx, k, half):
        return raw.at[c, ((x + dx) % 4) * 4 + (zl - k + 4) % 4, pl.ds(half * 8, 8)]

    def cot_sib(dx, k):
        return raw.at[1 - c, ((x + dx) % 4) * 4 + (zl - k + 4) % 4]

    def w_half(dz, dy, half):
        return weights.at[((zh + dz) % 4) * 4 + (y + dy) % 4, pl.ds(half * 2, 2)]

    def cot_out(k):
        own = cot_block(0, k)
        send(("ax", 1, k), own, own, xd[1])
        send(("ax", -1, k), own, own, xd[-1])
        send(("as", 0, k), own, own, sib)
        if k in DIRECT:
            send(("ax", 2, k), own, own, xd[2])

    def w_out_y(pieces):
        for way, half in pieces:
            block = w_half(0, 0, half)
            send(("by", way, 0, half), block, block, yd[way])

    def w_out_z(pieces):
        for way, half in pieces:
            block = w_half(0, 0, half)
            send(("bz", way, half), block, block, zd[way])

    def w_out_half(dz, half):
        block = w_half(dz, 0, half)
        for way in (1, -1):
            send(("by", way, dz, half), block, block, yd[way])

    def w_in(way, dz, half):
        block = w_half(dz, -way % 4, half)
        arrive(("by", way, dz, half), block)
        if (way, half) in FORWARD:
            send(("bf", way, dz), block, block, yd[way])

    def w_in_far(dz, way):
        arrive(("bf", way, dz), w_half(dz, 2, 0 if way == 1 else 1))

    def wz_in(way, half):
        block = w_half(-way, 0, half)
        arrive(("bz", way, half), block)
        if (way, half) in FORWARD:
            send(("bzf", way), block, block, zd[way])

    def wz_in_far(way):
        arrive(("bzf", way), w_half(2, 0, 0 if way == 1 else 1))

    own = cot_block(0, 0)
    for k in (1, 2, 3):
        send(("al", k), own, own, ld[k])
    cot_out(0)
    send("hid", hid_t.at[c], hid_t.at[c], sib)

    def cot_in_lo(k):
        arrive(("al", k), cot_block(0, k))
        cot_out(k)

    def cot_in_x(k, way):
        block = cot_block(-way, k)
        arrive(("ax", way, k), block)
        if k not in DIRECT:
            part_of = cot_half(-way, k, 0 if way == 1 else 1)
            send(("af", way, k), part_of, part_of, xd[way])
        send(("as", -way, k), block, block, sib)

    def cot_in_far(k):
        block = cot_block(2, k)
        if k in DIRECT:
            arrive(("ax", 2, k), block)
        else:
            arrive(("af", 1, k), cot_half(2, k, 0))
            arrive(("af", -1, k), cot_half(2, k, 1))
        send(("as", 2, k), block, block, sib)

    def repack(dx):
        def step(i, carry):
            core, pair = i // 2, ((x + dx) % 4) * 2 + i % 2
            first = raw[core, 2 * pair].astype(F32)
            second = raw[core, 2 * pair + 1].astype(F32)
            at = core * 8 + pair
            feats[0:16, at] = jnp.concatenate([first[:, :8], second[:, :8]], axis=1).astype(BF16)
            feats[16:32, at] = jnp.concatenate([first[:, 8:], second[:, 8:]], axis=1).astype(BF16)
            return carry

        lax.fori_loop(0, 4, step, 0)

    def from_sib(dx, ks):
        for k in ks:
            arrive(("as", dx, k), cot_sib(dx, k))

    def products(dz):
        def place(dy, carry):
            base = ((((zh + dz) % 4) * 4 + (y + dy) % 4) * 2 + c) * 4
            for q in range(4):
                hid = hid_ids[0, base + q]
                feat = feat_ids[0, base + q]
                left = jnp.concatenate([hid_t[0, hid], hid_t[1, hid]], axis=1)
                right = feats[feat].reshape(256, 128)
                prod[dz, dy, q] = jnp.dot(left, right, preferred_element_type=F32)
            return carry

        lax.fori_loop(0, 4, place, 0)

    def pair(half):
        return slice(2 * half, 2 * half + 2)

    def piece(half):
        return pl.ds(2 * half, 2)

    def c1(dz):
        for half, way in ((0, 1), (1, -1)):
            s1[dz, half] = prod[dz, 2, pair(half)].astype(BF16)
            send(("c1", dz, half), s1.at[dz, half], r1.at[dz, half], yd[way])

    def cp(dz):
        for half, way, dy in ((0, 1, 1), (1, -1, 3)):
            rest = 1 - half
            s2[dz, half, pair(rest)] = prod[dz, dy, pair(rest)].astype(BF16)
            send(("cp", dz, half), s2.at[dz, half, piece(rest)], r2.at[dz, half, piece(rest)], yd[way])

    def c2(dz, half):
        way, dy = ((1, 1), (-1, 3))[half]
        arrive(("c1", dz, half), r1.at[dz, half])
        s2[dz, half, pair(half)] = (prod[dz, dy, pair(half)] + r1[dz, half].astype(F32)).astype(BF16)
        send(("cs", dz, half), s2.at[dz, half, piece(half)], r2.at[dz, half, piece(half)], yd[way])

    def c3(dz, half):
        other_half = 1 - half
        arrive(("cp", dz, other_half), r2.at[dz, other_half, piece(half)])
        arrive(("cs", dz, half), r2.at[dz, half, piece(half)])
        rows = pair(half)
        part[dz, rows] = prod[dz, 0, rows] + r2[dz, 0, rows].astype(F32) + r2[dz, 1, rows].astype(F32)

    def d1(half):
        t1[half] = part[2, pair(half)].astype(BF16)
        send(("d1", half), t1.at[half], u1.at[half], zd[(1, -1)[half]])

    def d2_plain(dz):
        half, way = {1: (0, 1), 3: (1, -1)}[dz]
        rest = 1 - half
        t2[half, pair(rest)] = part[dz, pair(rest)].astype(BF16)
        send(("dp", half), t2.at[half, piece(rest)], u2.at[half, piece(rest)], zd[way])

    def d2(half):
        way, dz = ((1, 1), (-1, 3))[half]
        arrive(("d1", half), u1.at[half])
        t2[half, pair(half)] = (part[dz, pair(half)] + u1[half].astype(F32)).astype(BF16)
        send(("ds", half), t2.at[half, piece(half)], u2.at[half, piece(half)], zd[way])

    kept = count[0]

    def accumulate(dz, dy):
        at = ((zh + dz) % 4) * 4 + (y + dy) % 4
        base = (at * 2 + c) * 4
        picked = []
        for q in range(4):
            hid = jnp.where(base + q < kept, hid_ids[0, base + q], -1)
            picked.append(feats[feat_ids[0, base + q]].reshape(256, 128))
            block = weights[at, q]
            for j in range(7):
                spread[j * 128 : (j + 1) * 128, q * 128 : (q + 1) * 128] = jnp.where(
                    hid == j, block, jnp.zeros_like(block)
                )
        total[...] += lax.dot_general(
            jnp.concatenate(picked, axis=1), spread[...], (((1,), (1,)), ((), ())),
            preferred_element_type=F32,
        )

    def exchange():
        send("gh", total.at[pl.ds(pl.multiple_of((1 - c) * 128, 128), 128)], other, sib)

    def block_sums():
        for half in (0, 1):
            arrive(("dp", half), u2.at[half, piece(1 - half)])
            arrive(("ds", half), u2.at[half, piece(half)])
        for q in range(4):
            live = jnp.where(dp * 4 + q < kept, 1.0, 0.0)
            down[0, q] = (part[0, q] + u2[0, q].astype(F32) + u2[1, q].astype(F32)) * live

    def finish():
        arrive("gh", other)
        grad[...] = total[pl.ds(pl.multiple_of(c * 128, 128), 128), :] + other[...]

    w_out_y(OTHER)
    w_out_y(FORWARD)
    cot_in_x(0, 1)
    through_z()
    w_out_z(FORWARD)
    w_in(1, 0, 1)
    cot_in_x(0, -1)
    cot_in_lo(2)
    cot_in_lo(1)
    cot_in_far(0)
    cot_in_lo(3)
    w_in(1, 0, 0)
    cot_in_x(1, 1)
    cot_in_x(1, -1)
    w_in(-1, 0, 1)
    cot_in_x(2, 1)
    w_out_z(OTHER)
    cot_in_x(2, -1)
    wz_in(-1, 1)
    wz_in(1, 0)
    cot_in_x(3, 1)
    cot_in_x(3, -1)
    from_sib(0, (0, 1, 2, 3))
    repack(0)
    w_out_half(-1, 0)
    w_out_half(1, 1)
    cot_in_far(3)
    cot_in_far(1)
    cot_in_far(2)
    from_sib(1, (0, 1, 2, 3))
    repack(1)
    w_in_far(0, 1)
    arrive("hid", hid_t.at[1 - c])
    from_sib(-1, (0, 1, 2, 3))
    repack(3)
    from_sib(2, (0, 1, 2, 3))
    repack(2)
    products(2)
    c1(2)
    products(3)
    c1(3)
    products(1)
    w_in(-1, -1, 0)
    c1(1)
    cp(2)
    c2(2, 0)
    c2(2, 1)
    c2(3, 0)
    cp(3)
    cp(1)
    w_in_far(0, -1)
    w_in(1, 1, 1)
    accumulate(0, 0)
    c2(1, 1)
    wz_in_far(1)
    c3(2, 0)
    d1(0)
    w_in(-1, 0, 0)
    wz_in(-1, 0)
    c3(2, 1)
    d1(1)
    wz_in(1, 1)
    w_out_half(-1, 1)
    accumulate(0, 2)
    wz_in_far(-1)
    accumulate(1, 0)
    c2(3, 1)
    accumulate(2, 0)
    accumulate(0, 1)
    c2(1, 0)
    accumulate(0, 3)
    w_out_half(2, 0)
    c3(1, 1)
    w_in(1, -1, 1)
    w_out_half(2, 1)
    d2_plain(1)
    w_out_half(1, 0)
    c3(3, 0)
    d2_plain(3)
    c3(3, 1)
    w_in(1, 2, 0)
    w_in(-1, -1, 1)
    c3(1, 0)
    products(0)
    c1(0)
    w_in(-1, 2, 0)
    w_in(-1, 2, 1)
    w_in(1, 2, 1)
    d2(0)
    w_in(1, -1, 0)
    w_in(-1, 1, 1)
    w_in(-1, 1, 0)
    w_in(1, 1, 0)
    d2(1)
    accumulate(3, 0)
    accumulate(2, 1)
    c2(0, 0)
    accumulate(1, 1)
    c2(0, 1)
    cp(0)
    w_in_far(-1, -1)
    accumulate(1, 3)
    accumulate(3, 3)
    accumulate(3, 1)
    w_in_far(2, 1)
    accumulate(2, 3)
    w_in_far(2, -1)
    w_in_far(-1, 1)
    w_in_far(1, -1)
    accumulate(3, 2)
    w_in_far(1, 1)
    accumulate(1, 2)
    accumulate(2, 2)
    exchange()
    c3(0, 0)
    c3(0, 1)
    block_sums()
    finish()

    for copy in sent:
        copy.wait_send()
    assert len(names) == len(started) == len(arrived) <= send_sems.shape[0]


def per_device(gate_in, up_in, cotangent, w_down, block_hidden, block_feat, kept_counts):
    vmem = pl.BlockSpec(memory_space=pltpu.VMEM)
    hbm = pl.BlockSpec(memory_space=pl.ANY)
    smem = pl.BlockSpec(memory_space=pltpu.SMEM)
    copies = 128
    grad, down = pl.pallas_call(
        kernel,
        out_shape=(
            jax.ShapeDtypeStruct(gate_in.shape, F32),
            jax.ShapeDtypeStruct(w_down.shape, F32),
        ),
        in_specs=[hbm, hbm, hbm, hbm, smem, smem, smem],
        out_specs=(vmem, vmem),
        scratch_shapes=[
            pltpu.VMEM(gate_in.shape, BF16),
            pltpu.VMEM(up_in.shape, BF16),
            pltpu.VMEM(cotangent.shape, BF16),
            pltpu.VMEM((2, 16, 16, 16, 128), BF16),
            pltpu.VMEM((32, 16, 16, 128), BF16),
            pltpu.VMEM((2, 7, 128, 128), BF16),
            pltpu.VMEM((16, 4, 128, 128), BF16),
            pltpu.VMEM((896, 512), BF16),
            pltpu.VMEM((256, 896), F32),
            pltpu.VMEM((128, 896), F32),
            pltpu.VMEM((4, 4, 4, 128, 128), F32),
            pltpu.VMEM((4, 2, 2, 128, 128), BF16),
            pltpu.VMEM((4, 2, 2, 128, 128), BF16),
            pltpu.VMEM((4, 2, 4, 128, 128), BF16),
            pltpu.VMEM((4, 2, 4, 128, 128), BF16),
            pltpu.VMEM((4, 4, 128, 128), F32),
            pltpu.VMEM((2, 2, 128, 128), BF16),
            pltpu.VMEM((2, 2, 128, 128), BF16),
            pltpu.VMEM((2, 4, 128, 128), BF16),
            pltpu.VMEM((2, 4, 128, 128), BF16),
            pltpu.SemaphoreType.DMA((copies,)),
            pltpu.SemaphoreType.DMA((copies,)),
            pltpu.SemaphoreType.DMA((4,)),
            pltpu.SemaphoreType.REGULAR,
            pltpu.SemaphoreType.REGULAR,
        ],
        compiler_params=pltpu.CompilerParams(
            collective_id=0, has_side_effects=True, vmem_limit_bytes=60 * 2**20
        ),
    )(gate_in, up_in, cotangent, w_down, block_hidden, block_feat, kept_counts)
    g, u = gate_in.astype(F32), up_in.astype(F32)
    sigma = jax.nn.sigmoid(g)
    grad_gate = (grad * u * sigma * (1.0 + g * (1.0 - sigma))).astype(BF16)
    grad_up = (grad * (g * sigma)).astype(BF16)
    return grad_gate, grad_up, down.astype(BF16)


def solution(mesh):
    return jax.shard_map(
        per_device,
        mesh=mesh,
        in_specs=(
            P("dp", "tensor"),
            P("dp", "tensor"),
            P(("dp", "tensor"), None),
            P("tensor", "dp", None, None),
            P("tensor", None),
            P("tensor", None),
            P("tensor"),
        ),
        out_specs=(P("dp", "tensor"), P("dp", "tensor"), P("tensor", "dp", None, None)),
        check_vma=False,
    )
```
